32 devices in a mesh: groups: 2 (over y), dp: 8 (over z, x), pair: 2 (over core).
Axes of the slice: x: 2, y: 2, z: 4, core: 2. Of those that a mesh axis runs over, the one named last changes fastest.
Arguments:
- embeddings: bfloat16 [32768, 4096], P(('groups', 'dp'), 'pair'), parts along dimension 0, may hold values from -9 to 9
- pair_table: int32 [96, 2], P('groups'), parts along dimension 0, may hold values from -1 to 31, as said below
Outputs:
- smoothed: bfloat16 [32768, 4096], P(('groups', 'dp'), 'pair'), parts along dimension 0
- density: float32 [32768], P(('groups', 'dp')), parts along dimension 0
The draws below stay inside these ranges and needn't reach their ends.
There are 2 independent parts, one for each index of `groups`. The reference program is written for one: setup_inputs(seed, part) draws one part's arguments, and reference() takes and returns one part's arrays. A program takes and returns all parts, laid end to end along the dimension named above; each array names one. Nothing has to cross between parts.
Inputs may be any that keep to these rules, and one draw needn't show every extreme that they name: `pair_table`: each entry is a pair a <= b of block ids or (-1, -1) for an empty slot; no pair appears twice; every block g appears in the pair (g, g). Block g is held by index g // 4 of dp; the distinct blocks named in one table row all have different holders.
All inputs are finite; a program needn't handle non-finite values.
Results may differ from the reference program's by a relative error of at most 0.0049.
Values may be sent and summed in bfloat16 or wider, within the bound.
A program may use at most 256 MiB of HBM per device.

```python
import jax
import jax.numpy as jnp
from jax import lax

D = 4096
BLOCK = 512
BLK_DP = 4
PAIRS_DP = 6
NBLK = 32
N_DP = 8


def draw_embeddings(key, part):
    key = jax.random.fold_in(key, 5)
    total_rows = NBLK * BLOCK
    centers = jax.random.truncated_normal(jax.random.fold_in(key, 1), -3.0, 3.0, (16, D), jnp.float32)
    picked = jax.random.randint(jax.random.fold_in(key, 2), (total_rows,), 0, 16)
    jitter = jax.random.truncated_normal(jax.random.fold_in(key, 3), -3.0, 3.0, (total_rows, D), jnp.float32)
    scales = jnp.exp(jax.random.uniform(jax.random.fold_in(key, 4), (total_rows, 1), jnp.float32, -0.35, 0.35))
    return (scales * (centers[picked] + 0.5 * jitter)).astype(jnp.bfloat16)


def draw_pair_table(key, part):
    key = jax.random.fold_in(key, 11)
    holders = NBLK // BLK_DP
    lowest = max(2, holders // 4)
    highest = max(2, holders // 2 - 1)
    giant_size = jax.random.randint(jax.random.fold_in(key, 1), (), lowest, highest + 1)
    giant_stratum = jax.random.randint(jax.random.fold_in(key, 2), (), 0, BLK_DP)
    places = jnp.arange(holders, dtype=jnp.int32)
    upper_half = places[:, None] <= places[None, :]
    filled = jnp.full((holders * PAIRS_DP, 2), -1, jnp.int32)
    row_start = jnp.int32(0)
    for stratum in range(BLK_DP):
        holder_order = jax.random.permutation(jax.random.fold_in(key, 100 + stratum), holders).astype(jnp.int32)
        in_giant = (giant_stratum == stratum) & (places < giant_size)
        labels = jnp.where(in_giant, 0, places + 1)
        wanted = (upper_half & (labels[:, None] == labels[None, :])).reshape(-1).astype(jnp.int32)
        target = jnp.cumsum(wanted) - 1 + row_start * PAIRS_DP
        target = jnp.where(wanted > 0, target, holders * PAIRS_DP)
        block_ids = holder_order * BLK_DP + stratum
        first_ids = jnp.broadcast_to(block_ids[:, None], (holders, holders)).reshape(-1)
        second_ids = jnp.broadcast_to(block_ids[None, :], (holders, holders)).reshape(-1)
        couples = jnp.stack([jnp.minimum(first_ids, second_ids), jnp.maximum(first_ids, second_ids)], axis=1)
        filled = filled.at[target].set(couples, mode='drop')
        counted = jnp.sum(wanted)
        row_start = row_start + (counted + PAIRS_DP - 1) // PAIRS_DP
    shuffle = jax.random.permutation(jax.random.fold_in(key, 3), holders)
    return filled.reshape(holders, PAIRS_DP, 2)[shuffle].reshape(holders * PAIRS_DP, 2)


def setup_inputs(seed: int = 0, part: int = 0) -> dict:
    seeds = jax.random.split(jax.random.key(seed), 3)
    own_keys = jax.random.split(jax.random.fold_in(seeds[2], part), 3)
    return {
        "embeddings": draw_embeddings(jax.random.fold_in(jax.random.fold_in(seeds[2], part), 71), part),
        "pair_table": draw_pair_table(jax.random.fold_in(jax.random.fold_in(seeds[2], part), 71), part),
    }


kernel_scale = 2.0


def reference(embeddings, pair_table):
    width = embeddings.shape[1]
    block_list = embeddings.reshape(NBLK, BLOCK, width)
    entries = pair_table.reshape(N_DP, PAIRS_DP, 2)

    def pair_table_row(carry, row_entries):
        weighted, density = carry
        row_sums = jnp.zeros((NBLK, BLOCK, width), jnp.float32)
        row_mass = jnp.zeros((NBLK, BLOCK), jnp.float32)
        for column_index in range(PAIRS_DP):
            first_id = row_entries[column_index, 0]
            second_id = row_entries[column_index, 1]
            is_valid = first_id >= 0
            left_index = jnp.maximum(first_id, 0).astype(jnp.int32)
            right_index = jnp.maximum(second_id, 0).astype(jnp.int32)
            left_block = lax.dynamic_index_in_dim(block_list, left_index, 0, keepdims=False)
            right_block = lax.dynamic_index_in_dim(block_list, right_index, 0, keepdims=False)
            left_norm = jnp.sum(jnp.square(left_block.astype(jnp.float32)), axis=1)
            right_norm = jnp.sum(jnp.square(right_block.astype(jnp.float32)), axis=1)
            crossed = jnp.dot(left_block, right_block.T, preferred_element_type=jnp.float32)
            distance = left_norm[:, None] + right_norm[None, :] - 2.0 * crossed
            kernel = jnp.exp(-kernel_scale * distance / D).astype(jnp.bfloat16)
            kernel_wide = kernel.astype(jnp.float32)
            weight_first = is_valid.astype(jnp.float32)
            second_weight = (is_valid & (first_id != second_id)).astype(jnp.float32)
            toward_first = jnp.dot(kernel, right_block, preferred_element_type=jnp.float32)
            toward_second = jnp.dot(kernel.T, left_block, preferred_element_type=jnp.float32)
            row_sums = row_sums.at[left_index].add(weight_first * toward_first)
            row_sums = row_sums.at[right_index].add(second_weight * toward_second)
            row_mass = row_mass.at[left_index].add(weight_first * jnp.sum(kernel_wide, axis=1))
            row_mass = row_mass.at[right_index].add(second_weight * jnp.sum(kernel_wide, axis=0))
        rounded = lax.optimization_barrier(row_sums.astype(jnp.bfloat16)).astype(jnp.float32)
        return (weighted + rounded, density + row_mass), None

    start = (jnp.zeros((NBLK, BLOCK, width), jnp.float32), jnp.zeros((NBLK, BLOCK), jnp.float32))
    (weighted, density), unused = lax.scan(pair_table_row, start, entries)
    smoothed = (weighted / density[:, :, None]).astype(jnp.bfloat16).reshape(NBLK * BLOCK, width)
    return smoothed, density.reshape(-1)
```

```python
import itertools

import jax
import jax.numpy as jnp
from jax import lax
from jax.sharding import PartitionSpec as P

D = 4096
BLOCK = 512
BLK_DP = 4
PAIRS_DP = 6
TRIPLE_HOLDERS = 8


kernel_scale = 2.0


def kernel_of(distance):
    return jnp.exp(-kernel_scale * distance / D).astype(jnp.bfloat16)


def sum_over_pair(partial):
    members = lax.axis_size("pair")
    step = 1
    while step < members:
        partial = partial + lax.ppermute(
            partial, "pair", [(i, i ^ step) for i in range(members)]
        )
        step *= 2
    return partial


def listed(chosen, capacity):
    place = jnp.cumsum(chosen.astype(jnp.int32)) - 1
    hit = chosen[None, :] & (place[None, :] == jnp.arange(capacity)[:, None])
    index = jnp.arange(chosen.shape[0])
    return jnp.sum(jnp.where(hit, index[None, :], 0), axis=1), jnp.sum(chosen.astype(jnp.int32))


def plan(tables, holders):
    rows = tables.shape[0] // PAIRS_DP
    entries = tables.reshape(rows, PAIRS_DP, 2)
    first_ids, second_ids = entries[:, :, 0], entries[:, :, 1]
    off = (first_ids >= 0) & (first_ids != second_ids)
    low = jnp.min(jnp.where(off, first_ids, holders * BLK_DP), axis=1)
    high = jnp.max(jnp.where(off, second_ids, -1), axis=1)
    middle = jnp.sum(jnp.where(off, first_ids + second_ids, 0), axis=1) // 2 - low - high
    lo, mi, hi = low[:, None], middle[:, None], high[:, None]
    edge = (
        ((first_ids == lo) & (second_ids == mi))
        | ((first_ids == lo) & (second_ids == hi))
        | ((first_ids == mi) & (second_ids == hi))
    )
    triple = (jnp.sum(off.astype(jnp.int32), axis=1) == 3) & jnp.all(edge | ~off, axis=1)
    triple = triple & (low < middle) & (middle < high)
    if holders > TRIPLE_HOLDERS:
        triple = jnp.zeros_like(triple)
    triple_rows, triple_count = listed(triple, rows)
    swap = (off & ~triple[:, None]).reshape(-1)
    swap_entries, swap_count = listed(swap, rows * (PAIRS_DP - BLK_DP))
    named = jnp.stack([low, middle, high], axis=1)
    return (named, triple_rows, triple_count), (tables, swap_entries, swap_count)


def rank_of(holder):
    if len(holder) == 2:
        return holder[1] * (holder[1] - 1) // 2 + holder[0]
    return (
        holder[2] * (holder[2] - 1) * (holder[2] - 2) // 6
        + holder[1] * (holder[1] - 1) // 2
        + holder[0]
    )


def per_device(embeddings, pair_table):
    holders = lax.axis_size("dp")
    myself = lax.axis_index("dp")
    resident_rows, columns = embeddings.shape
    blocks = embeddings.reshape(BLK_DP, BLOCK, columns)
    my_group = lax.axis_index("groups")
    tables = lax.all_gather(pair_table, "groups", axis=0, tiled=True)
    triples, swaps = plan(tables, holders)

    def swapper(i, j):
        return lambda block: lax.ppermute(block, "dp", [(i, j), (j, i)])

    def rotator(i, j, k):
        ring = [(i, j), (j, k), (k, i)]
        back = [(b, a) for a, b in ring]
        return lambda block: jnp.concatenate(
            [lax.ppermute(block, "dp", ring), lax.ppermute(block, "dp", back)]
        )

    def combos(size):
        return sorted(itertools.combinations(range(holders), size), key=lambda c: c[::-1])

    swappers = [swapper(*c) for c in combos(2)]
    rotators = []
    if holders <= TRIPLE_HOLDERS:
        rotators = [rotator(*c) for c in combos(3)]

    crossed = jnp.einsum("brf,bqf->brq", blocks, blocks, preferred_element_type=jnp.float32)
    crossed = sum_over_pair(crossed)
    eye = jnp.eye(BLOCK, dtype=jnp.bool_)
    norm = jnp.sum(jnp.where(eye, crossed, 0.0), axis=2)
    kernel = kernel_of(norm[:, :, None] + norm[:, None, :] - 2.0 * crossed)
    mass = jnp.sum(kernel.astype(jnp.float32), axis=2)
    sums = jnp.einsum("brq,bqf->brf", kernel, blocks, preferred_element_type=jnp.float32)

    def work(task, movers, size):
        named, order, count = task
        group_rows = named.shape[0] // lax.axis_size("groups")

        def step(at, carry):
            sums, mass = carry
            ids = [named[order[at], k] for k in range(size)]
            holder = [i // BLK_DP for i in ids]
            own, mine = jnp.int32(0), jnp.bool_(False)
            for k in range(size):
                own = jnp.where(holder[k] == myself, ids[k] % BLK_DP, own)
                mine = mine | (holder[k] == myself)
            mine = mine & (order[at] // group_rows == my_group)
            left = lax.dynamic_index_in_dim(blocks, own, 0, keepdims=False)
            right = lax.switch(rank_of(holder), movers, left)
            left_norm = lax.dynamic_index_in_dim(norm, own, 0, keepdims=False)
            right_norm = jnp.sum(jnp.square(right.astype(jnp.float32)), axis=1)
            cross = jnp.einsum("rf,qf->rq", left, right, preferred_element_type=jnp.float32)
            distance = left_norm[:, None] + sum_over_pair(right_norm[None, :] - 2.0 * cross)
            kernel = jnp.where(mine, kernel_of(distance), jnp.bfloat16(0))
            toward = jnp.einsum("rq,qf->rf", kernel, right, preferred_element_type=jnp.float32)
            sums = sums.at[own].add(toward)
            mass = mass.at[own].add(jnp.sum(kernel.astype(jnp.float32), axis=1))
            return sums, mass

        return lambda carry: lax.fori_loop(0, count, step, carry)

    carry = (sums, mass)
    if rotators:
        carry = work(triples, rotators, 3)(carry)
    sums, density = work(swaps, swappers, 2)(carry)
    smoothed = (sums / density[:, :, None]).astype(jnp.bfloat16)
    return (smoothed.reshape(resident_rows, columns), density.reshape(-1))


def solution(mesh):
    placed = (P(("groups", "dp"), "pair"), P("groups", None))
    return jax.shard_map(
        per_device,
        mesh=mesh,
        in_specs=placed,
        out_specs=(P(("groups", "dp"), "pair"), P(("groups", "dp"))),
        check_vma=False,
    )
```

```python
import itertools

import jax
import jax.numpy as jnp
from jax import lax
from jax.sharding import PartitionSpec as P

D = 4096
BLOCK = 512
BLK_DP = 4
PAIRS_DP = 6
TRIPLE_HOLDERS = 8


kernel_scale = 2.0


def kernel_of(distance):
    return jnp.exp(-kernel_scale * distance / D).astype(jnp.bfloat16)


def sum_over_pair(partial):
    members = lax.axis_size("pair")
    step = 1
    while step < members:
        partial = partial + lax.ppermute(
            partial, "pair", [(i, i ^ step) for i in range(members)]
        )
        step *= 2
    return partial


def listed(chosen, capacity):
    place = jnp.cumsum(chosen.astype(jnp.int32)) - 1
    hit = chosen[None, :] & (place[None, :] == jnp.arange(capacity)[:, None])
    index = jnp.arange(chosen.shape[0])
    return jnp.sum(jnp.where(hit, index[None, :], 0), axis=1), jnp.sum(chosen.astype(jnp.int32))


def plan(tables, holders):
    rows = tables.shape[0] // PAIRS_DP
    entries = tables.reshape(rows, PAIRS_DP, 2)
    first_ids, second_ids = entries[:, :, 0], entries[:, :, 1]
    off = (first_ids >= 0) & (first_ids != second_ids)
    low = jnp.min(jnp.where(off, first_ids, holders * BLK_DP), axis=1)
    high = jnp.max(jnp.where(off, second_ids, -1), axis=1)
    middle = jnp.sum(jnp.where(off, first_ids + second_ids, 0), axis=1) // 2 - low - high
    lo, mi, hi = low[:, None], middle[:, None], high[:, None]
    edge = (
        ((first_ids == lo) & (second_ids == mi))
        | ((first_ids == lo) & (second_ids == hi))
        | ((first_ids == mi) & (second_ids == hi))
    )
    triple = (jnp.sum(off.astype(jnp.int32), axis=1) == 3) & jnp.all(edge | ~off, axis=1)
    triple = triple & (low < middle) & (middle < high)
    if holders > TRIPLE_HOLDERS:
        triple = jnp.zeros_like(triple)
    triple_rows, triple_count = listed(triple, rows)
    swap = (off & ~triple[:, None]).reshape(-1)
    swap_entries, swap_count = listed(swap, rows * (PAIRS_DP - BLK_DP))
    named = jnp.stack([low, middle, high], axis=1)
    return (named, triple_rows, triple_count), (tables, swap_entries, swap_count)


def rank_of(holder):
    if len(holder) == 2:
        return holder[1] * (holder[1] - 1) // 2 + holder[0]
    return (
        holder[2] * (holder[2] - 1) * (holder[2] - 2) // 6
        + holder[1] * (holder[1] - 1) // 2
        + holder[0]
    )


def per_device(embeddings, pair_table):
    holders = lax.axis_size("dp")
    myself = lax.axis_index("dp")
    resident_rows, columns = embeddings.shape
    blocks = embeddings.reshape(BLK_DP, BLOCK, columns)
    my_group = lax.axis_index("groups")
    tables = lax.all_gather(pair_table, "groups", axis=0, tiled=True)
    triples, swaps = plan(tables, holders)

    def swapper(i, j):
        return lambda block: (lax.ppermute(block, "dp", [(i, j), (j, i)]),)

    def rotator(i, j, k):
        ring = [(i, j), (j, k), (k, i)]
        back = [(b, a) for a, b in ring]
        return lambda block: (
            lax.ppermute(block, "dp", ring),
            lax.ppermute(block, "dp", back),
        )

    def combos(size):
        return sorted(itertools.combinations(range(holders), size), key=lambda c: c[::-1])

    swappers = [swapper(*c) for c in combos(2)]
    rotators = []
    if holders <= TRIPLE_HOLDERS:
        rotators = [rotator(*c) for c in combos(3)]

    crossed = jnp.einsum("brf,bqf->brq", blocks, blocks, preferred_element_type=jnp.float32)
    crossed = sum_over_pair(crossed)
    eye = jnp.eye(BLOCK, dtype=jnp.bool_)
    norm = jnp.sum(jnp.where(eye, crossed, 0.0), axis=2)
    kernel = kernel_of(norm[:, :, None] + norm[:, None, :] - 2.0 * crossed)
    mass = jnp.sum(kernel.astype(jnp.float32), axis=2)
    sums = jnp.einsum("brq,bqf->brf", kernel, blocks, preferred_element_type=jnp.float32)

    def work(task, movers, size):
        named, order, count = task
        group_rows = named.shape[0] // lax.axis_size("groups")

        def step(at, carry):
            sums, mass = carry
            ids = [named[order[at], k] for k in range(size)]
            holder = [i // BLK_DP for i in ids]
            own, mine = jnp.int32(0), jnp.bool_(False)
            for k in range(size):
                own = jnp.where(holder[k] == myself, ids[k] % BLK_DP, own)
                mine = mine | (holder[k] == myself)
            mine = mine & (order[at] // group_rows == my_group)
            left = lax.dynamic_index_in_dim(blocks, own, 0, keepdims=False)
            right = jnp.concatenate(lax.switch(rank_of(holder), movers, left))
            left_norm = lax.dynamic_index_in_dim(norm, own, 0, keepdims=False)
            right_norm = jnp.sum(jnp.square(right.astype(jnp.float32)), axis=1)
            cross = jnp.einsum("rf,qf->rq", left, right, preferred_element_type=jnp.float32)
            distance = left_norm[:, None] + sum_over_pair(right_norm[None, :] - 2.0 * cross)
            kernel = jnp.where(mine, kernel_of(distance), jnp.bfloat16(0))
            toward = jnp.einsum("rq,qf->rf", kernel, right, preferred_element_type=jnp.float32)
            sums = sums.at[own].add(toward)
            mass = mass.at[own].add(jnp.sum(kernel.astype(jnp.float32), axis=1))
            return sums, mass

        return lambda carry: lax.fori_loop(0, count, step, carry)

    carry = (sums, mass)
    if rotators:
        carry = work(triples, rotators, 3)(carry)
    sums, density = work(swaps, swappers, 2)(carry)
    smoothed = (sums / density[:, :, None]).astype(jnp.bfloat16)
    return (smoothed.reshape(resident_rows, columns), density.reshape(-1))


def solution(mesh):
    placed = (P(("groups", "dp"), "pair"), P("groups", None))
    return jax.shard_map(
        per_device,
        mesh=mesh,
        in_specs=placed,
        out_specs=(P(("groups", "dp"), "pair"), P(("groups", "dp"))),
        check_vma=False,
    )
```

```python
import itertools

import jax
import jax.numpy as jnp
from jax import lax
from jax.sharding import PartitionSpec as P

D = 4096
BLOCK = 512
BLK_DP = 4
PAIRS_DP = 6
TRIPLE_HOLDERS = 8


kernel_scale = 2.0


def kernel_of(distance):
    return jnp.exp(-kernel_scale * distance / D).astype(jnp.bfloat16)


def sum_over_pair(partial):
    members = lax.axis_size("pair")
    step = 1
    while step < members:
        partial = partial + lax.ppermute(
            partial, "pair", [(i, i ^ step) for i in range(members)]
        )
        step *= 2
    return partial


def listed(chosen, capacity):
    place = jnp.cumsum(chosen.astype(jnp.int32)) - 1
    hit = chosen[None, :] & (place[None, :] == jnp.arange(capacity)[:, None])
    index = jnp.arange(chosen.shape[0])
    return jnp.sum(jnp.where(hit, index[None, :], 0), axis=1), jnp.sum(chosen.astype(jnp.int32))


def plan(tables, holders):
    rows = tables.shape[0] // PAIRS_DP
    entries = tables.reshape(rows, PAIRS_DP, 2)
    first_ids, second_ids = entries[:, :, 0], entries[:, :, 1]
    off = (first_ids >= 0) & (first_ids != second_ids)
    low = jnp.min(jnp.where(off, first_ids, holders * BLK_DP), axis=1)
    high = jnp.max(jnp.where(off, second_ids, -1), axis=1)
    middle = jnp.sum(jnp.where(off, first_ids + second_ids, 0), axis=1) // 2 - low - high
    lo, mi, hi = low[:, None], middle[:, None], high[:, None]
    edge = (
        ((first_ids == lo) & (second_ids == mi))
        | ((first_ids == lo) & (second_ids == hi))
        | ((first_ids == mi) & (second_ids == hi))
    )
    triple = (jnp.sum(off.astype(jnp.int32), axis=1) == 3) & jnp.all(edge | ~off, axis=1)
    triple = triple & (low < middle) & (middle < high)
    if holders > TRIPLE_HOLDERS:
        triple = jnp.zeros_like(triple)
    triple_rows, triple_count = listed(triple, rows)
    swap = (off & ~triple[:, None]).reshape(-1)
    swap_entries, swap_count = listed(swap, rows * (PAIRS_DP - BLK_DP))
    named = jnp.stack([low, middle, high], axis=1)
    return (named, triple_rows, triple_count), (tables, swap_entries, swap_count)


def rank_of(holder):
    if len(holder) == 2:
        return holder[1] * (holder[1] - 1) // 2 + holder[0]
    return (
        holder[2] * (holder[2] - 1) * (holder[2] - 2) // 6
        + holder[1] * (holder[1] - 1) // 2
        + holder[0]
    )


def per_device(embeddings, pair_table):
    holders = lax.axis_size("dp")
    myself = lax.axis_index("dp")
    resident_rows, columns = embeddings.shape
    blocks = embeddings.reshape(BLK_DP, BLOCK, columns)
    my_group = lax.axis_index("groups")
    tables = lax.all_gather(pair_table, "groups", axis=0, tiled=True)
    triples, swaps = plan(tables, holders)

    def swapper(i, j):
        return lambda block: (lax.ppermute(block, "dp", [(i, j), (j, i)]),)

    def rotator(i, j, k):
        ring = [(i, j), (j, k), (k, i)]
        back = [(b, a) for a, b in ring]
        return lambda block: (
            lax.ppermute(block, "dp", ring),
            lax.ppermute(block, "dp", back),
        )

    def combos(size):
        return sorted(itertools.combinations(range(holders), size), key=lambda c: c[::-1])

    swappers = [swapper(*c) for c in combos(2)]
    rotators = []
    if holders <= TRIPLE_HOLDERS:
        rotators = [rotator(*c) for c in combos(3)]

    crossed = jnp.einsum("brf,bqf->brq", blocks, blocks, preferred_element_type=jnp.float32)
    crossed = sum_over_pair(crossed)
    eye = jnp.eye(BLOCK, dtype=jnp.bool_)
    norm = jnp.sum(jnp.where(eye, crossed, 0.0), axis=2)
    kernel = kernel_of(norm[:, :, None] + norm[:, None, :] - 2.0 * crossed)
    mass = jnp.sum(kernel.astype(jnp.float32), axis=2)
    sums = jnp.einsum("brq,bqf->brf", kernel, blocks, preferred_element_type=jnp.float32)

    def work(task, movers, size):
        named, order, count = task
        group_rows = named.shape[0] // lax.axis_size("groups")

        def step(at, carry):
            sums, mass = carry
            ids = [named[order[at], k] for k in range(size)]
            holder = [i // BLK_DP for i in ids]
            own, mine = jnp.int32(0), jnp.bool_(False)
            for k in range(size):
                own = jnp.where(holder[k] == myself, ids[k] % BLK_DP, own)
                mine = mine | (holder[k] == myself)
            mine = mine & (order[at] // group_rows == my_group)
            left = blocks[0]
            for b in range(1, BLK_DP):
                left = jnp.where(own == b, blocks[b], left)
            right = jnp.concatenate(lax.switch(rank_of(holder), movers, left))
            left_norm = lax.dynamic_index_in_dim(norm, own, 0, keepdims=False)
            right_norm = jnp.sum(jnp.square(right.astype(jnp.float32)), axis=1)
            cross = jnp.einsum("rf,qf->rq", left, right, preferred_element_type=jnp.float32)
            distance = left_norm[:, None] + sum_over_pair(right_norm[None, :] - 2.0 * cross)
            kernel = jnp.where(mine, kernel_of(distance), jnp.bfloat16(0))
            toward = jnp.einsum("rq,qf->rf", kernel, right, preferred_element_type=jnp.float32)
            sums = sums.at[own].add(toward)
            mass = mass.at[own].add(jnp.sum(kernel.astype(jnp.float32), axis=1))
            return sums, mass

        return lambda carry: lax.fori_loop(0, count, step, carry)

    carry = (sums, mass)
    if rotators:
        carry = work(triples, rotators, 3)(carry)
    sums, density = work(swaps, swappers, 2)(carry)
    smoothed = (sums / density[:, :, None]).astype(jnp.bfloat16)
    return (smoothed.reshape(resident_rows, columns), density.reshape(-1))


def solution(mesh):
    placed = (P(("groups", "dp"), "pair"), P("groups", None))
    return jax.shard_map(
        per_device,
        mesh=mesh,
        in_specs=placed,
        out_specs=(P(("groups", "dp"), "pair"), P(("groups", "dp"))),
        check_vma=False,
    )
```
